32 devices in a mesh: rep: 8 (over y, x, core), shard: 4 (over z).
Axes of the slice: x: 2, y: 2, z: 4, core: 2. Of those that a mesh axis runs over, the one named last changes fastest.
Arguments:
- gradients: bfloat16 [8, 96, 2560], P(None, 'shard')
- momentum: float32 [8, 96, 2560], P(None, 'shard'), may hold values from -60 to 60
Outputs:
- updates: bfloat16 [8, 96, 2560], P(None, 'shard', 'rep')
- new_momentum: float32 [8, 96, 2560], P(None, 'shard')
The draws below stay inside these ranges and needn't reach their ends.
All inputs are finite; a program needn't handle non-finite values.
Results may differ from the reference program's by a relative error of at most 0.0014.
Values may be sent and summed in bfloat16 or wider, within the bound.
A program may use at most 64 MiB of HBM per device.

```python
import math
import jax
import jax.numpy as jnp
from jax import lax

E = 96
D = 2560
ITERS = 5
MAT = 8


def draw_gradients(key, part):
    keys = jax.random.split(key, 3)
    row_scale = jnp.exp(jax.random.uniform(keys[1], (MAT, E, 1), jnp.float32) * math.log(10.0))
    col_scale = jnp.exp(jax.random.uniform(keys[2], (MAT, 1, D), jnp.float32) * math.log(10.0))
    noise = jax.random.normal(keys[0], (MAT, E, D), jnp.float32)
    values = noise * row_scale * col_scale
    return values.astype(jnp.bfloat16)


def steps_of(stream_key, dims, cuts, least, high):
    def one(position, blocks):
        steps = jax.random.uniform(jax.random.fold_in(jax.random.fold_in(stream_key, 6), position), (blocks,), jnp.float32, least / len(cuts), high / len(cuts))
        return jnp.repeat(jnp.exp(steps), dims[position] // blocks).reshape((-1,) + (1,) * (len(dims) - position - 1))

    loudness = one(*cuts[0])
    for cut in cuts[1:]:
        loudness = loudness * one(*cut)
    return loudness


def centred(stream_key, dims, deviation, limit, cuts=(), dtype=jnp.bfloat16):
    entries = deviation * jax.random.normal(stream_key, dims, jnp.float32)
    if cuts:
        entries = entries * steps_of(stream_key, dims, cuts, -0.22, 0.18)
    return jnp.clip(entries, -limit, limit).astype(dtype)


def setup_inputs(seed: int = 0) -> dict:
    splits = jax.random.split(jax.random.key(seed), 3)
    gradients = draw_gradients(jax.random.fold_in(splits[2], 71), 0)
    momentum = centred(splits[1], (MAT, E, D), 10.0, 60.0, ((1, 4),), jnp.float32)
    return {"gradients": gradients, "momentum": momentum}


momentum_decay = 0.95
norm_floor = 1e-07
quintic_terms = (3.4445, -4.775, 2.0315)

def newton_schulz(effective):
    iterate = effective / (jnp.sqrt(jnp.sum(effective * effective)) + norm_floor)
    for turn in range(ITERS):
        gram_mat = jnp.dot(iterate, iterate.T, precision=lax.Precision.HIGHEST, preferred_element_type=jnp.float32)
        poly_mat = quintic_terms[1] * gram_mat + quintic_terms[2] * jnp.dot(gram_mat, gram_mat, precision=lax.Precision.HIGHEST, preferred_element_type=jnp.float32)
        iterate = quintic_terms[0] * iterate + jnp.dot(poly_mat, iterate, precision=lax.Precision.HIGHEST, preferred_element_type=jnp.float32)
    return iterate

def reference(gradients, momentum):
    update_scale = 0.2 * math.sqrt(max(E, D))
    gradient_values = gradients.astype(jnp.float32)
    new_momentum = momentum_decay * momentum + gradient_values
    effective = gradient_values + momentum_decay * new_momentum

    def single(operand):
        return (update_scale * newton_schulz(operand)).astype(jnp.bfloat16)
    updates = lax.map(single, effective)
    return (updates, new_momentum)
```

```python
import math

import jax
import jax.numpy as jnp
from jax import lax
from jax.sharding import PartitionSpec as P

ITERS = 5
momentum_decay = 0.95
norm_floor = 1e-07
quintic_terms = (3.4445, -4.775, 2.0315)


def mm(a, b):
    return jnp.einsum("kij,kjl->kil", a, b, precision=lax.Precision.HIGHEST)


def schulz_factor(gram, scale):
    total = jnp.trace(gram, axis1=1, axis2=2)[:, None, None]
    inverse = 1.0 / (jnp.sqrt(total) + norm_floor)
    g = jnp.where(inverse > 0, gram * inverse * inverse, 0.0)
    eye = jnp.eye(gram.shape[-1], dtype=jnp.float32)
    a, b, c = quintic_terms
    q = None
    for turn in range(ITERS):
        poly = a * eye + b * g + c * mm(g, g)
        q = poly if q is None else mm(poly, q)
        if turn < ITERS - 1:
            g = mm(poly, mm(poly, g))
    return q * (scale * inverse)


def per_device_plain(gradients, momentum):
    rows, width = gradients.shape[1:]
    scale = 0.2 * math.sqrt(max(rows * lax.axis_size("shard"), width))
    replicas = lax.axis_size("rep")
    grads = gradients.astype(jnp.float32)
    new_momentum = momentum_decay * momentum + grads
    effective = grads + momentum_decay * new_momentum
    cols = width // replicas
    mine = lax.dynamic_slice_in_dim(effective, lax.axis_index("rep") * cols, cols, 2)
    whole = lax.all_to_all(mine, "shard", split_axis=0, concat_axis=1, tiled=True)
    gram = jnp.einsum("kij,klj->kil", whole, whole, precision=lax.Precision.HIGHEST)
    factor = schulz_factor(lax.psum(gram, "rep"), scale)
    out = mm(factor, whole).astype(jnp.bfloat16)
    return lax.all_to_all(out, "shard", split_axis=1, concat_axis=0, tiled=True), new_momentum


def solution(mesh):
    in_specs = (P(None, "shard", None), P(None, "shard", None))
    out_specs = (P(None, "shard", "rep"), P(None, "shard", None))
    return jax.shard_map(
        per_device_plain, mesh=mesh, in_specs=in_specs, out_specs=out_specs, check_vma=False
    )
```

```python
import functools
import math

import jax
import jax.numpy as jnp
from jax import lax
from jax.experimental import pallas as pl
from jax.experimental.pallas import tpu as pltpu
from jax.sharding import PartitionSpec as P

ITERS = 5
LANES = 128
momentum_decay = 0.95
norm_floor = 1e-07
quintic_terms = (3.4445, -4.775, 2.0315)
MESH = pl.DeviceIdType.MESH


def mm(a, b):
    return jnp.einsum("kij,kjl->kil", a, b, precision=lax.Precision.HIGHEST)


def schulz_factor(gram, scale):
    total = jnp.trace(gram, axis1=1, axis2=2)[:, None, None]
    inverse = jnp.where(total < jnp.inf, 1.0 / (jnp.sqrt(total) + norm_floor), 0.0)
    g = jnp.where(inverse > 0, gram * inverse * inverse, 0.0)
    eye = jnp.eye(gram.shape[-1], dtype=jnp.float32)
    a, b, c = quintic_terms
    q = None
    for turn in range(ITERS):
        poly = a * eye + b * g + c * mm(g, g)
        q = poly if q is None else mm(poly, q)
        if turn < ITERS - 1:
            g = mm(poly, mm(poly, g))
    return q * (scale * inverse)


def per_device_plain(gradients, momentum):
    rows, width = gradients.shape[1:]
    scale = 0.2 * math.sqrt(max(rows * lax.axis_size("shard"), width))
    replicas = lax.axis_size("rep")
    grads = gradients.astype(jnp.float32)
    new_momentum = momentum_decay * momentum + grads
    effective = grads + momentum_decay * new_momentum
    cols = width // replicas
    mine = lax.dynamic_slice_in_dim(effective, lax.axis_index("rep") * cols, cols, 2)
    whole = lax.all_to_all(mine, "shard", split_axis=0, concat_axis=1, tiled=True)
    gram = jnp.einsum("kij,klj->kil", whole, whole, precision=lax.Precision.HIGHEST)
    factor = schulz_factor(lax.psum(gram, "rep"), scale)
    out = mm(factor, whole).astype(jnp.bfloat16)
    return lax.all_to_all(out, "shard", split_axis=1, concat_axis=0, tiled=True), new_momentum


def split(x):
    high = x.astype(jnp.bfloat16)
    return high, (x - high.astype(jnp.float32)).astype(jnp.bfloat16)


def left(x):
    return jnp.concatenate(split(x), axis=1)


def right(x):
    pair = jnp.concatenate(split(x), axis=1)
    return jnp.concatenate([pair, pair], axis=0)


def product(lhs, rhs):
    n = rhs.shape[1] // 2
    out = jnp.dot(lhs, rhs, preferred_element_type=jnp.float32)
    return out[:, :n] + out[:, n:]


def kernel(shards, per, groups, g_hbm, m_hbm, upd_ref, newm_hbm,
           gc, mc, gf, mf, nf, send, x_ref, xs, part, parts, stage, recv,
           chunk_sem, full_sem, store_sem, s1, r1, s2, r2, s3, r3):
    mats, rows, width = g_hbm.shape
    chunk = width // groups
    cols = chunk // per
    n = shards * rows
    scale = 0.2 * math.sqrt(max(n, width))
    rep, s = lax.axis_index("rep"), lax.axis_index("shard")
    j, c = rep // per, rep % per

    def plane(k):
        return lax.rem(s + k, shards)

    at = pl.ds(pl.multiple_of(j * chunk, LANES), chunk)
    chunk_loads = []
    for k in range(shards):
        mat = plane(k) * per + c
        pair = (pltpu.make_async_copy(g_hbm.at[mat, :, at], gc.at[k], chunk_sem.at[0, k]),
                pltpu.make_async_copy(m_hbm.at[mat, :, at], mc.at[k], chunk_sem.at[1, k]))
        chunk_loads.append(pair)
    order = list(range(1, shards)) + [0]
    for k in order:
        for copy in chunk_loads[k]:
            copy.start()

    barrier = pltpu.get_barrier_semaphore()
    peers = []
    for k in range(shards):
        for d in range(per):
            if k or d:
                peers.append((j * per + lax.rem(c + d, per), plane(k)))
    for k in range(1, groups):
        peers.append((lax.rem(j + k, groups) * per + c, s))
    for peer in peers:
        pl.semaphore_signal(barrier, inc=1, device_id=peer, device_id_type=MESH)

    full_loads = []
    for mat in range(mats):
        pair = (pltpu.make_async_copy(g_hbm.at[mat], gf.at[mat], full_sem.at[0, mat]),
                pltpu.make_async_copy(m_hbm.at[mat], mf.at[mat], full_sem.at[1, mat]))
        full_loads.append(pair)
        for copy in pair:
            copy.start()

    def effective(k):
        for copy in chunk_loads[k]:
            copy.wait()
        grads = gc[k].astype(jnp.float32)
        return grads + momentum_decay * (momentum_decay * mc[k] + grads)

    for k in range(1, shards):
        send[k] = effective(k)
    pl.semaphore_wait(barrier, len(peers))
    first = []
    for k in range(1, shards):
        copy = pltpu.make_async_remote_copy(
            src_ref=send.at[k], dst_ref=x_ref.at[k], send_sem=s1.at[k], recv_sem=r1.at[k],
            device_id=(rep, plane(k)), device_id_type=MESH)
        copy.start()
        first.append(copy)
    x_ref[0] = effective(0)

    stores = []
    for mat in range(mats):
        for copy in full_loads[mat]:
            copy.wait()
        nf[mat] = momentum_decay * mf[mat] + gf[mat].astype(jnp.float32)
        copy = pltpu.make_async_copy(nf.at[mat], newm_hbm.at[mat], store_sem.at[mat])
        copy.start()
        stores.append(copy)

    for copy in first:
        copy.wait_recv()
    x = x_ref[...].reshape(n, chunk)
    high, low = split(x)
    pad = jnp.zeros((LANES - n, chunk), jnp.bfloat16)
    xs[...] = jnp.concatenate([high, pad, low, pad], axis=0)
    quad = lax.dot_general(xs[...], xs[...], (((1,), (1,)), ((), ())),
                           preferred_element_type=jnp.float32)
    mine = (quad[:LANES, :LANES] + quad[LANES:, LANES:]) + (quad[:LANES, LANES:] + quad[LANES:, :LANES])
    part[...] = mine[:n]
    second = []
    for k in range(1, groups):
        copy = pltpu.make_async_remote_copy(
            src_ref=part, dst_ref=parts.at[k], send_sem=s2.at[k], recv_sem=r2.at[k],
            device_id=(lax.rem(j + k, groups) * per + c, s), device_id_type=MESH)
        copy.start()
        second.append(copy)
    gram = mine[:n]
    for k, copy in zip(range(1, groups), second):
        copy.wait_recv()
        gram = gram + parts[k]
    gram = jnp.concatenate([gram, jnp.zeros((LANES - n, LANES), jnp.float32)], axis=0)

    diagonal = (lax.broadcasted_iota(jnp.int32, (LANES, LANES), 0)
                == lax.broadcasted_iota(jnp.int32, (LANES, LANES), 1))
    total = jnp.sum(jnp.where(diagonal, gram, 0.0), axis=(0, 1), keepdims=True)
    inverse = jnp.where(total < jnp.inf, 1.0 / (jnp.sqrt(total) + norm_floor), 0.0)
    g = jnp.where(inverse > 0, gram * inverse * inverse, 0.0)
    a, b, c2 = quintic_terms
    eye = jnp.where(diagonal, a, 0.0)
    q = None
    for turn in range(ITERS):
        g_right = right(g)
        poly = (eye + b * g) + c2 * product(left(g), g_right)
        poly_left = left(poly)
        if turn < ITERS - 1:
            g = product(poly_left, right(product(poly_left, g_right)))
        q = poly if q is None else product(poly_left, right(q))
    q_high, q_low = split((q * (scale * inverse))[:n])
    lhs = jnp.concatenate([jnp.concatenate([q_high, q_high], axis=1),
                           jnp.concatenate([q_low, q_low], axis=1)], axis=0)
    both = jnp.dot(lhs, xs[...], preferred_element_type=jnp.float32)
    out = jnp.where(inverse > 0, both[:n] + both[n:], 0.0)

    half = LANES // 2
    low_lanes = lax.broadcasted_iota(jnp.int32, (rows, LANES), 1) < half
    main = cols - half
    for k in range(shards):
        block = out[k * rows:(k + 1) * rows]
        tiles = [block[:, t * LANES:(t + 1) * LANES] for t in range(chunk // LANES)]
        middle = len(tiles) // 2
        turned = [pltpu.roll(t, half, 1) for t in tiles[middle:]]
        shifted = [jnp.where(low_lanes, p, t) for p, t in zip(turned[:-1], turned[1:])]
        for d, (body, tail) in enumerate(((tiles[:middle], tiles[middle]), (shifted, turned[-1]))):
            extra = jnp.concatenate(
                [jnp.where(low_lanes[:8], tail[:8], pltpu.roll(tail[8:16], half, 1)), tail[16:24]], axis=1)
            packed = jnp.concatenate([jnp.concatenate(body, axis=1), extra], axis=0)
            stage[k, d] = packed.astype(jnp.bfloat16)
    third = {}
    for k in [*range(1, shards), 0]:
        for d in range(per):
            if k or d:
                core = lax.rem(c + d, per)
                copy = pltpu.make_async_remote_copy(
                    src_ref=stage.at[k, core], dst_ref=recv.at[k, d],
                    send_sem=s3.at[k, d], recv_sem=r3.at[k, d],
                    device_id=(j * per + core, plane(shards - k)), device_id_type=MESH)
                copy.start()
                third[k, d] = copy

    for k in range(shards):
        for d in range(per):
            if k or d:
                third[k, d].wait_recv()
                block = recv[k, d].astype(jnp.float32)
            else:
                block = stage[0, c].astype(jnp.float32)
            mat = plane(k) * per + lax.rem(c + per - d, per)
            lanes = block[rows:, :LANES]
            tail = jnp.concatenate([lanes, pltpu.roll(lanes, half, 1), block[rows:, LANES:2 * LANES]], axis=0)
            upd_ref[mat, :, :main] = block[:rows].astype(jnp.bfloat16)
            upd_ref[mat, :, main:] = tail[:, :half].astype(jnp.bfloat16)
    for copy in stores:
        copy.wait()
    for copy in first + second + list(third.values()):
        copy.wait_send()


def per_device_kernel(shards, per, groups, gradients, momentum):
    mats, rows, width = gradients.shape
    chunk = width // groups
    cols = chunk // per
    n = shards * rows
    packed = (shards, per, rows + 8, cols - LANES // 2)
    f32, bf16, dma = jnp.float32, jnp.bfloat16, pltpu.SemaphoreType.DMA
    return pl.pallas_call(
        functools.partial(kernel, shards, per, groups),
        out_shape=(jax.ShapeDtypeStruct((mats, rows, cols), bf16),
                   jax.ShapeDtypeStruct((mats, rows, width), f32)),
        in_specs=[pl.BlockSpec(memory_space=pl.ANY)] * 2,
        out_specs=(pl.BlockSpec(memory_space=pltpu.VMEM), pl.BlockSpec(memory_space=pl.ANY)),
        scratch_shapes=[
            pltpu.VMEM((shards, rows, chunk), bf16),
            pltpu.VMEM((shards, rows, chunk), f32),
            pltpu.VMEM((mats, rows, width), bf16),
            pltpu.VMEM((mats, rows, width), f32),
            pltpu.VMEM((mats, rows, width), f32),
            pltpu.VMEM((shards, rows, chunk), f32),
            pltpu.VMEM((shards, rows, chunk), f32),
            pltpu.VMEM((2 * LANES, chunk), bf16),
            pltpu.VMEM((n, LANES), f32),
            pltpu.VMEM((groups, n, LANES), f32),
            pltpu.VMEM(packed, bf16),
            pltpu.VMEM(packed, bf16),
            dma((2, shards)), dma((2, mats)), dma((mats,)),
            dma((shards,)), dma((shards,)), dma((groups,)), dma((groups,)),
            dma((shards, per)), dma((shards, per)),
        ],
        compiler_params=pltpu.CompilerParams(
            collective_id=0, has_side_effects=True, vmem_limit_bytes=40 * 2**20),
    )(gradients, momentum)


def kernel_fits(shards, replicas, mats, n, width):
    if mats % shards or n % shards:
        return False
    per, rows = mats // shards, n // shards
    if per != 2 or rows != 24 or n > LANES or replicas % per:
        return False
    chunk = width * per // replicas
    return chunk % (2 * LANES) == LANES and chunk >= 5 * LANES


def solution(mesh):
    shards, replicas = mesh.shape["shard"], mesh.shape["rep"]

    def per_device(gradients, momentum):
        mats, rows, width = gradients.shape
        if kernel_fits(shards, replicas, mats, rows * shards, width):
            per = mats // shards
            return per_device_kernel(shards, per, replicas // per, gradients, momentum)
        return per_device_plain(gradients, momentum)

    in_specs = (P(None, "shard", None), P(None, "shard", None))
    out_specs = (P(None, "shard", "rep"), P(None, "shard", None))
    return jax.shard_map(
        per_device, mesh=mesh, in_specs=in_specs, out_specs=out_specs, check_vma=False
    )
```

```python
import functools
import math

import jax
import jax.numpy as jnp
from jax import lax
from jax.experimental import pallas as pl
from jax.experimental.pallas import tpu as pltpu
from jax.sharding import PartitionSpec as P

ITERS = 5
LANES = 128
momentum_decay = 0.95
norm_floor = 1e-07
quintic_terms = (3.4445, -4.775, 2.0315)
MESH = pl.DeviceIdType.MESH


def mm(a, b):
    return jnp.einsum("kij,kjl->kil", a, b, precision=lax.Precision.HIGHEST)


def schulz_factor(gram, scale):
    total = jnp.trace(gram, axis1=1, axis2=2)[:, None, None]
    inverse = jnp.where(total < jnp.inf, 1.0 / (jnp.sqrt(total) + norm_floor), 0.0)
    g = jnp.where(inverse > 0, gram * inverse * inverse, 0.0)
    eye = jnp.eye(gram.shape[-1], dtype=jnp.float32)
    a, b, c = quintic_terms
    q = None
    for turn in range(ITERS):
        poly = a * eye + b * g + c * mm(g, g)
        q = poly if q is None else mm(poly, q)
        if turn < ITERS - 1:
            g = mm(poly, mm(poly, g))
    return q * (scale * inverse)


def per_device_plain(gradients, momentum):
    rows, width = gradients.shape[1:]
    scale = 0.2 * math.sqrt(max(rows * lax.axis_size("shard"), width))
    replicas = lax.axis_size("rep")
    grads = gradients.astype(jnp.float32)
    new_momentum = momentum_decay * momentum + grads
    effective = grads + momentum_decay * new_momentum
    cols = width // replicas
    mine = lax.dynamic_slice_in_dim(effective, lax.axis_index("rep") * cols, cols, 2)
    whole = lax.all_to_all(mine, "shard", split_axis=0, concat_axis=1, tiled=True)
    gram = jnp.einsum("kij,klj->kil", whole, whole, precision=lax.Precision.HIGHEST)
    factor = schulz_factor(lax.psum(gram, "rep"), scale)
    out = mm(factor, whole).astype(jnp.bfloat16)
    return lax.all_to_all(out, "shard", split_axis=1, concat_axis=0, tiled=True), new_momentum


def split(x):
    high = x.astype(jnp.bfloat16)
    return high, (x - high.astype(jnp.float32)).astype(jnp.bfloat16)


def left(x):
    return jnp.concatenate(split(x), axis=1)


def right(x):
    pair = jnp.concatenate(split(x), axis=1)
    return jnp.concatenate([pair, pair], axis=0)


def product(lhs, rhs):
    n = rhs.shape[1] // 2
    out = jnp.dot(lhs, rhs, preferred_element_type=jnp.float32)
    return out[:, :n] + out[:, n:]


def kernel(shards, per, groups, scale, eff_ref, out_ref,
           x_ref, xs, part, parts, stage, recv, s1, r1, s2, r2, s3, r3):
    _, rows, chunk = eff_ref.shape
    cols = chunk // per
    n = shards * rows
    rep, s = lax.axis_index("rep"), lax.axis_index("shard")
    j, c = rep // per, rep % per

    def plane(k):
        return lax.rem(s + k, shards)

    barrier = pltpu.get_barrier_semaphore()
    peers = []
    for k in range(shards):
        for d in range(per):
            if k or d:
                peers.append((j * per + lax.rem(c + d, per), plane(k)))
    for k in range(1, groups):
        peers.append((lax.rem(j + k, groups) * per + c, s))
    for peer in peers:
        pl.semaphore_signal(barrier, inc=1, device_id=peer, device_id_type=MESH)

    pl.semaphore_wait(barrier, len(peers))
    first = []
    for k in range(1, shards):
        copy = pltpu.make_async_remote_copy(
            src_ref=eff_ref.at[plane(k)], dst_ref=x_ref.at[k], send_sem=s1.at[k], recv_sem=r1.at[k],
            device_id=(rep, plane(k)), device_id_type=MESH)
        copy.start()
        first.append(copy)
    x_ref[0] = eff_ref[s]

    for copy in first:
        copy.wait_recv()
    x = x_ref[...].reshape(n, chunk)
    high, low = split(x)
    pad = jnp.zeros((LANES - n, chunk), jnp.bfloat16)
    xs[...] = jnp.concatenate([high, pad, low, pad], axis=0)
    quad = lax.dot_general(xs[...], xs[...], (((1,), (1,)), ((), ())),
                           preferred_element_type=jnp.float32)
    mine = (quad[:LANES, :LANES] + quad[LANES:, LANES:]) + (quad[:LANES, LANES:] + quad[LANES:, :LANES])
    part[...] = mine[:n]
    second = []
    for k in range(1, groups):
        copy = pltpu.make_async_remote_copy(
            src_ref=part, dst_ref=parts.at[k], send_sem=s2.at[k], recv_sem=r2.at[k],
            device_id=(lax.rem(j + k, groups) * per + c, s), device_id_type=MESH)
        copy.start()
        second.append(copy)
    gram = mine[:n]
    for k, copy in zip(range(1, groups), second):
        copy.wait_recv()
        gram = gram + parts[k]
    gram = jnp.concatenate([gram, jnp.zeros((LANES - n, LANES), jnp.float32)], axis=0)

    diagonal = (lax.broadcasted_iota(jnp.int32, (LANES, LANES), 0)
                == lax.broadcasted_iota(jnp.int32, (LANES, LANES), 1))
    total = jnp.sum(jnp.where(diagonal, gram, 0.0), axis=(0, 1), keepdims=True)
    inverse = jnp.where(total < jnp.inf, 1.0 / (jnp.sqrt(total) + norm_floor), 0.0)
    g = jnp.where(inverse > 0, gram * inverse * inverse, 0.0)
    a, b, c2 = quintic_terms
    eye = jnp.where(diagonal, a, 0.0)
    q = None
    for turn in range(ITERS):
        g_right = right(g)
        poly = (eye + b * g) + c2 * product(left(g), g_right)
        poly_left = left(poly)
        if turn < ITERS - 1:
            g = product(poly_left, right(product(poly_left, g_right)))
        q = poly if q is None else product(poly_left, right(q))
    q_high, q_low = split((q * (scale * inverse))[:n])
    lhs = jnp.concatenate([jnp.concatenate([q_high, q_high], axis=1),
                           jnp.concatenate([q_low, q_low], axis=1)], axis=0)
    both = jnp.dot(lhs, xs[...], preferred_element_type=jnp.float32)
    out = jnp.where(inverse > 0, both[:n] + both[n:], 0.0)

    half = LANES // 2
    low_lanes = lax.broadcasted_iota(jnp.int32, (rows, LANES), 1) < half
    for k in range(shards):
        block = out[k * rows:(k + 1) * rows]
        tiles = [block[:, t * LANES:(t + 1) * LANES] for t in range(chunk // LANES)]
        middle = len(tiles) // 2
        turned = [pltpu.roll(t, half, 1) for t in tiles[middle:]]
        shifted = [jnp.where(low_lanes, p, t) for p, t in zip(turned[:-1], turned[1:])]
        for d, (body, tail) in enumerate(((tiles[:middle], tiles[middle]), (shifted, turned[-1]))):
            extra = jnp.concatenate(
                [jnp.where(low_lanes[:8], tail[:8], pltpu.roll(tail[8:16], half, 1)), tail[16:24]], axis=1)
            packed = jnp.concatenate([jnp.concatenate(body, axis=1), extra], axis=0)
            stage[k, d] = packed.astype(jnp.bfloat16)
    third = {}
    for k in [*range(1, shards), 0]:
        for d in range(per):
            if k or d:
                core = lax.rem(c + d, per)
                copy = pltpu.make_async_remote_copy(
                    src_ref=stage.at[k, core], dst_ref=recv.at[k, d],
                    send_sem=s3.at[k, d], recv_sem=r3.at[k, d],
                    device_id=(j * per + core, plane(shards - k)), device_id_type=MESH)
                copy.start()
                third[k, d] = copy

    out_ref[0, 0] = stage[0, c]
    for k in range(shards):
        for d in range(per):
            if k or d:
                third[k, d].wait_recv()
                out_ref[k, d] = recv[k, d]
    for copy in first + second + list(third.values()):
        copy.wait_send()


def finish(shards, per, packed_ref, g_ref, m_ref, upd_hbm, newm_hbm, nf, upd, sems):
    mats, rows, width = g_ref.shape
    cols = upd.shape[2]
    half = LANES // 2
    main = cols - half
    rep, s = lax.axis_index("rep"), lax.axis_index("shard")
    c = rep % per
    copies = []
    for mat in range(mats):
        nf[mat] = momentum_decay * m_ref[mat] + g_ref[mat].astype(jnp.float32)
        copies.append(pltpu.make_async_copy(nf.at[mat], newm_hbm.at[mat], sems.at[mat]))
        copies[-1].start()
    for k in range(shards):
        for d in range(per):
            block = packed_ref[k, d].astype(jnp.float32)
            mat = lax.rem(s + k, shards) * per + lax.rem(c + per - d, per)
            lanes = block[rows:, :LANES]
            tail = jnp.concatenate([lanes, pltpu.roll(lanes, half, 1), block[rows:, LANES:2 * LANES]], axis=0)
            upd[mat, :, :main] = block[:rows].astype(jnp.bfloat16)
            upd[mat, :, main:] = tail[:, :half].astype(jnp.bfloat16)
    copies.append(pltpu.make_async_copy(upd, upd_hbm, sems.at[mats]))
    copies[-1].start()
    for copy in copies:
        copy.wait()


def per_device_kernel(shards, per, groups, gradients, momentum):
    mats, rows, width = gradients.shape
    chunk = width // groups
    cols = chunk // per
    n = shards * rows
    scale = 0.2 * math.sqrt(max(n, width))
    packed = (shards, per, rows + 8, cols - LANES // 2)
    f32, bf16, dma = jnp.float32, jnp.bfloat16, pltpu.SemaphoreType.DMA
    vmem, anywhere = pl.BlockSpec(memory_space=pltpu.VMEM), pl.BlockSpec(memory_space=pl.ANY)
    rep = lax.axis_index("rep")

    def chunk_of(x):
        x = x.reshape(shards, per, rows, width)
        x = lax.dynamic_slice(x, (0, rep % per, 0, rep // per * chunk), (shards, 1, rows, chunk))
        return x.reshape(shards, rows, chunk)

    grads = chunk_of(gradients).astype(f32)
    effective = grads + momentum_decay * (momentum_decay * chunk_of(momentum) + grads)
    blocks = pl.pallas_call(
        functools.partial(kernel, shards, per, groups, scale),
        out_shape=jax.ShapeDtypeStruct(packed, bf16),
        in_specs=[vmem],
        out_specs=vmem,
        scratch_shapes=[
            pltpu.VMEM((shards, rows, chunk), f32),
            pltpu.VMEM((2 * LANES, chunk), bf16),
            pltpu.VMEM((n, LANES), f32),
            pltpu.VMEM((groups, n, LANES), f32),
            pltpu.VMEM(packed, bf16),
            pltpu.VMEM(packed, bf16),
            dma((shards,)), dma((shards,)), dma((groups,)), dma((groups,)),
            dma((shards, per)), dma((shards, per)),
        ],
        cost_estimate=pl.CostEstimate(flops=20_000_000_000, bytes_accessed=1_000_000, transcendentals=0),
        compiler_params=pltpu.CompilerParams(
            collective_id=0, has_side_effects=True, vmem_limit_bytes=24 * 2**20),
    )(effective)
    return pl.pallas_call(
        functools.partial(finish, shards, per),
        out_shape=(jax.ShapeDtypeStruct((mats, rows, cols), bf16),
                   jax.ShapeDtypeStruct((mats, rows, width), f32)),
        in_specs=[vmem] * 3,
        out_specs=(anywhere, anywhere),
        scratch_shapes=[
            pltpu.VMEM((mats, rows, width), f32),
            pltpu.VMEM((mats, rows, cols), bf16),
            dma((mats + 1,)),
        ],
        compiler_params=pltpu.CompilerParams(vmem_limit_bytes=24 * 2**20),
    )(blocks, gradients, momentum)


def kernel_fits(shards, replicas, mats, n, width):
    if mats % shards or n % shards:
        return False
    per, rows = mats // shards, n // shards
    if per != 2 or rows != 24 or n > LANES or replicas % per:
        return False
    chunk = width * per // replicas
    return chunk % (2 * LANES) == LANES and chunk >= 5 * LANES


def solution(mesh):
    shards, replicas = mesh.shape["shard"], mesh.shape["rep"]

    def per_device(gradients, momentum):
        mats, rows, width = gradients.shape
        if kernel_fits(shards, replicas, mats, rows * shards, width):
            per = mats // shards
            return per_device_kernel(shards, per, replicas // per, gradients, momentum)
        return per_device_plain(gradients, momentum)

    in_specs = (P(None, "shard", None), P(None, "shard", None))
    out_specs = (P(None, "shard", "rep"), P(None, "shard", None))
    return jax.shard_map(
        per_device, mesh=mesh, in_specs=in_specs, out_specs=out_specs, check_vma=False
    )
```

```python
import functools
import math

import jax
import jax.numpy as jnp
from jax import lax
from jax.experimental import pallas as pl
from jax.experimental.pallas import tpu as pltpu
from jax.sharding import PartitionSpec as P

ITERS = 5
LANES = 128
momentum_decay = 0.95
norm_floor = 1e-07
quintic_terms = (3.4445, -4.775, 2.0315)
MESH = pl.DeviceIdType.MESH


def mm(a, b):
    return jnp.einsum("kij,kjl->kil", a, b, precision=lax.Precision.HIGHEST)


def schulz_factor(gram, scale):
    total = jnp.trace(gram, axis1=1, axis2=2)[:, None, None]
    inverse = jnp.where(total < jnp.inf, 1.0 / (jnp.sqrt(total) + norm_floor), 0.0)
    g = jnp.where(inverse > 0, gram * inverse * inverse, 0.0)
    eye = jnp.eye(gram.shape[-1], dtype=jnp.float32)
    a, b, c = quintic_terms
    q = None
    for turn in range(ITERS):
        poly = a * eye + b * g + c * mm(g, g)
        q = poly if q is None else mm(poly, q)
        if turn < ITERS - 1:
            g = mm(poly, mm(poly, g))
    return q * (scale * inverse)


def per_device_plain(gradients, momentum):
    rows, width = gradients.shape[1:]
    scale = 0.2 * math.sqrt(max(rows * lax.axis_size("shard"), width))
    replicas = lax.axis_size("rep")
    grads = gradients.astype(jnp.float32)
    new_momentum = momentum_decay * momentum + grads
    effective = grads + momentum_decay * new_momentum
    cols = width // replicas
    mine = lax.dynamic_slice_in_dim(effective, lax.axis_index("rep") * cols, cols, 2)
    whole = lax.all_to_all(mine, "shard", split_axis=0, concat_axis=1, tiled=True)
    gram = jnp.einsum("kij,klj->kil", whole, whole, precision=lax.Precision.HIGHEST)
    factor = schulz_factor(lax.psum(gram, "rep"), scale)
    out = mm(factor, whole).astype(jnp.bfloat16)
    return lax.all_to_all(out, "shard", split_axis=1, concat_axis=0, tiled=True), new_momentum


def split(x):
    high = x.astype(jnp.bfloat16)
    return high, (x - high.astype(jnp.float32)).astype(jnp.bfloat16)


def left(x):
    return jnp.concatenate(split(x), axis=1)


def right(x):
    pair = jnp.concatenate(split(x), axis=1)
    return jnp.concatenate([pair, pair], axis=0)


def product(lhs, rhs):
    n = rhs.shape[1] // 2
    out = jnp.dot(lhs, rhs, preferred_element_type=jnp.float32)
    return out[:, :n] + out[:, n:]


def partner(s, k):
    for b in range(k.bit_length()):
        if k >> b & 1:
            s = s + (1 << b) * (1 - 2 * (s // (1 << b) % 2))
    return s


def far_first(shards):
    return sorted(range(1, shards), key=lambda k: -k)


def kernel(shards, per, groups, scale, eff_ref, out_ref,
           x_ref, xs, part, parts, stage, recv, s1, r1, s2, r2, s3, r3):
    _, rows, chunk = eff_ref.shape
    cols = chunk // per
    n = shards * rows
    rep, s = lax.axis_index("rep"), lax.axis_index("shard")
    j, c = rep // per, rep % per

    def plane(k):
        return partner(s, k)

    barrier = pltpu.get_barrier_semaphore()
    peers = []
    for k in range(shards):
        for d in range(per):
            if k or d:
                peers.append((j * per + lax.rem(c + d, per), plane(k)))
    for k in range(1, groups):
        peers.append((lax.rem(j + k, groups) * per + c, s))
    for peer in peers:
        pl.semaphore_signal(barrier, inc=1, device_id=peer, device_id_type=MESH)

    pl.semaphore_wait(barrier, len(peers))
    first = []
    for k in far_first(shards):
        copy = pltpu.make_async_remote_copy(
            src_ref=eff_ref.at[plane(k)], dst_ref=x_ref.at[k], send_sem=s1.at[k], recv_sem=r1.at[k],
            device_id=(rep, plane(k)), device_id_type=MESH)
        copy.start()
        first.append(copy)
    x_ref[0] = eff_ref[s]

    for copy in first:
        copy.wait_recv()
    x = x_ref[...].reshape(n, chunk)
    high, low = split(x)
    pad = jnp.zeros((LANES - n, chunk), jnp.bfloat16)
    xs[...] = jnp.concatenate([high, pad, low, pad], axis=0)
    quad = lax.dot_general(xs[...], xs[...], (((1,), (1,)), ((), ())),
                           preferred_element_type=jnp.float32)
    mine = (quad[:LANES, :LANES] + quad[LANES:, LANES:]) + (quad[:LANES, LANES:] + quad[LANES:, :LANES])
    part[...] = mine[:n]
    second = []
    for k in range(1, groups):
        copy = pltpu.make_async_remote_copy(
            src_ref=part, dst_ref=parts.at[k], send_sem=s2.at[k], recv_sem=r2.at[k],
            device_id=(lax.rem(j + k, groups) * per + c, s), device_id_type=MESH)
        copy.start()
        second.append(copy)
    gram = mine[:n]
    for k, copy in zip(range(1, groups), second):
        copy.wait_recv()
        gram = gram + parts[k]
    gram = jnp.concatenate([gram, jnp.zeros((LANES - n, LANES), jnp.float32)], axis=0)

    diagonal = (lax.broadcasted_iota(jnp.int32, (LANES, LANES), 0)
                == lax.broadcasted_iota(jnp.int32, (LANES, LANES), 1))
    total = jnp.sum(jnp.where(diagonal, gram, 0.0), axis=(0, 1), keepdims=True)
    inverse = jnp.where(total < jnp.inf, 1.0 / (jnp.sqrt(total) + norm_floor), 0.0)
    g = jnp.where(inverse > 0, gram * inverse * inverse, 0.0)
    a, b, c2 = quintic_terms
    eye = jnp.where(diagonal, a, 0.0)
    q = None
    for turn in range(ITERS):
        g_right = right(g)
        poly = (eye + b * g) + c2 * product(left(g), g_right)
        poly_left = left(poly)
        if turn < ITERS - 1:
            g = product(poly_left, right(product(poly_left, g_right)))
        q = poly if q is None else product(poly_left, right(q))
    q_high, q_low = split((q * (scale * inverse))[:n])
    lhs = jnp.concatenate([jnp.concatenate([q_high, q_high], axis=1),
                           jnp.concatenate([q_low, q_low], axis=1)], axis=0)
    both = jnp.dot(lhs, xs[...], preferred_element_type=jnp.float32)
    out = jnp.where(inverse > 0, both[:n] + both[n:], 0.0)

    half = LANES // 2
    low_lanes = lax.broadcasted_iota(jnp.int32, (rows, LANES), 1) < half
    for k in range(shards):
        block = out[k * rows:(k + 1) * rows]
        tiles = [block[:, t * LANES:(t + 1) * LANES] for t in range(chunk // LANES)]
        middle = len(tiles) // 2
        turned = [pltpu.roll(t, half, 1) for t in tiles[middle:]]
        shifted = [jnp.where(low_lanes, p, t) for p, t in zip(turned[:-1], turned[1:])]
        for d, (body, tail) in enumerate(((tiles[:middle], tiles[middle]), (shifted, turned[-1]))):
            extra = jnp.concatenate(
                [jnp.where(low_lanes[:8], tail[:8], pltpu.roll(tail[8:16], half, 1)), tail[16:24]], axis=1)
            packed = jnp.concatenate([jnp.concatenate(body, axis=1), extra], axis=0)
            stage[k, d] = packed.astype(jnp.bfloat16)
    third = {}
    for k in [*far_first(shards), 0]:
        for d in range(per):
            if k or d:
                core = lax.rem(c + d, per)
                copy = pltpu.make_async_remote_copy(
                    src_ref=stage.at[k, core], dst_ref=recv.at[k, d],
                    send_sem=s3.at[k, d], recv_sem=r3.at[k, d],
                    device_id=(j * per + core, plane(k)), device_id_type=MESH)
                copy.start()
                third[k, d] = copy

    out_ref[0, 0] = stage[0, c]
    for k in range(shards):
        for d in range(per):
            if k or d:
                third[k, d].wait_recv()
                out_ref[k, d] = recv[k, d]
    for copy in first + second + list(third.values()):
        copy.wait_send()


def finish(shards, per, packed_ref, g_ref, m_ref, upd_hbm, newm_hbm, nf, upd, sems):
    mats, rows, width = g_ref.shape
    cols = upd.shape[2]
    half = LANES // 2
    main = cols - half
    rep, s = lax.axis_index("rep"), lax.axis_index("shard")
    c = rep % per
    copies = []
    for mat in range(mats):
        nf[mat] = momentum_decay * m_ref[mat] + g_ref[mat].astype(jnp.float32)
        copies.append(pltpu.make_async_copy(nf.at[mat], newm_hbm.at[mat], sems.at[mat]))
        copies[-1].start()
    for k in range(shards):
        for d in range(per):
            block = packed_ref[k, d].astype(jnp.float32)
            mat = partner(s, k) * per + lax.rem(c + per - d, per)
            lanes = block[rows:, :LANES]
            tail = jnp.concatenate([lanes, pltpu.roll(lanes, half, 1), block[rows:, LANES:2 * LANES]], axis=0)
            upd[mat, :, :main] = block[:rows].astype(jnp.bfloat16)
            upd[mat, :, main:] = tail[:, :half].astype(jnp.bfloat16)
    copies.append(pltpu.make_async_copy(upd, upd_hbm, sems.at[mats]))
    copies[-1].start()
    for copy in copies:
        copy.wait()


def per_device_kernel(shards, per, groups, gradients, momentum):
    mats, rows, width = gradients.shape
    chunk = width // groups
    cols = chunk // per
    n = shards * rows
    scale = 0.2 * math.sqrt(max(n, width))
    packed = (shards, per, rows + 8, cols - LANES // 2)
    f32, bf16, dma = jnp.float32, jnp.bfloat16, pltpu.SemaphoreType.DMA
    vmem, anywhere = pl.BlockSpec(memory_space=pltpu.VMEM), pl.BlockSpec(memory_space=pl.ANY)
    rep = lax.axis_index("rep")

    def chunk_of(x):
        x = x.reshape(shards, per, rows, width)
        x = lax.dynamic_slice(x, (0, rep % per, 0, rep // per * chunk), (shards, 1, rows, chunk))
        return x.reshape(shards, rows, chunk)

    grads = chunk_of(gradients).astype(f32)
    effective = grads + momentum_decay * (momentum_decay * chunk_of(momentum) + grads)
    blocks = pl.pallas_call(
        functools.partial(kernel, shards, per, groups, scale),
        out_shape=jax.ShapeDtypeStruct(packed, bf16),
        in_specs=[vmem],
        out_specs=vmem,
        scratch_shapes=[
            pltpu.VMEM((shards, rows, chunk), f32),
            pltpu.VMEM((2 * LANES, chunk), bf16),
            pltpu.VMEM((n, LANES), f32),
            pltpu.VMEM((groups, n, LANES), f32),
            pltpu.VMEM(packed, bf16),
            pltpu.VMEM(packed, bf16),
            dma((shards,)), dma((shards,)), dma((groups,)), dma((groups,)),
            dma((shards, per)), dma((shards, per)),
        ],
        cost_estimate=pl.CostEstimate(flops=20_000_000_000, bytes_accessed=1_000_000, transcendentals=0),
        compiler_params=pltpu.CompilerParams(
            collective_id=0, has_side_effects=True, vmem_limit_bytes=24 * 2**20),
    )(effective)
    return pl.pallas_call(
        functools.partial(finish, shards, per),
        out_shape=(jax.ShapeDtypeStruct((mats, rows, cols), bf16),
                   jax.ShapeDtypeStruct((mats, rows, width), f32)),
        in_specs=[vmem] * 3,
        out_specs=(anywhere, anywhere),
        scratch_shapes=[
            pltpu.VMEM((mats, rows, width), f32),
            pltpu.VMEM((mats, rows, cols), bf16),
            dma((mats + 1,)),
        ],
        compiler_params=pltpu.CompilerParams(vmem_limit_bytes=24 * 2**20),
    )(blocks, gradients, momentum)


def kernel_fits(shards, replicas, mats, n, width):
    if mats % shards or n % shards:
        return False
    per, rows = mats // shards, n // shards
    if shards & (shards - 1):
        return False
    if per != 2 or rows != 24 or n > LANES or replicas % per:
        return False
    chunk = width * per // replicas
    return chunk % (2 * LANES) == LANES and chunk >= 5 * LANES


def solution(mesh):
    shards, replicas = mesh.shape["shard"], mesh.shape["rep"]

    def per_device(gradients, momentum):
        mats, rows, width = gradients.shape
        if kernel_fits(shards, replicas, mats, rows * shards, width):
            per = mats // shards
            return per_device_kernel(shards, per, replicas // per, gradients, momentum)
        return per_device_plain(gradients, momentum)

    in_specs = (P(None, "shard", None), P(None, "shard", None))
    out_specs = (P(None, "shard", "rep"), P(None, "shard", None))
    return jax.shard_map(
        per_device, mesh=mesh, in_specs=in_specs, out_specs=out_specs, check_vma=False
    )
```
